32 devices in a mesh: grp: 2 (over x), doc: 16 (over z, y, core).
Axes of the slice: x: 2, y: 2, z: 4, core: 2. Of those that a mesh axis runs over, the one named last changes fastest.
Arguments:
- doc_grads: bfloat16 [16, 512, 32768], P('doc', 'grp'), parts along dimension 1, may hold values from -6 to 6
- query_grads: bfloat16 [16, 2048, 32768], P('doc', 'grp'), parts along dimension 1, may hold values from -180 to 180
Outputs:
- influence: float32 [8192, 1024], P(('grp', 'doc')), parts along dimension 0
The draws below stay inside these ranges and needn't reach their ends.
There are 2 independent parts, one for each index of `grp`. The reference program is written for one: setup_inputs(seed, part) draws one part's arguments, and reference() takes and returns one part's arrays. A program takes and returns all parts, laid end to end along the dimension named above; each array names one. Nothing has to cross between parts.
All inputs are finite; a program needn't handle non-finite values.
Results may differ from the reference program's by a relative error of at most 0.0003.
Values may be sent and summed in bfloat16 or wider, within the bound.
A program may use at most 256 MiB of HBM per device.

```python
import math
import jax
import jax.numpy as jnp
from jax import lax

K = 131072
QRY_GRP = 1024
DOC_GRP = 256
KSPL = 4
KBLK = 32768
NQ = 4096
NDOC = 1024


def draw_doc_grads(key, part):
    key = jax.random.fold_in(key, 11)
    noise_key, row_key, col_key = jax.random.split(key, 3)
    values = jax.random.normal(noise_key, (4, KSPL, DOC_GRP, KBLK), jnp.float32)
    values = jnp.clip(values, -6.0, 6.0)
    row_scale = jnp.exp(jax.random.uniform(row_key, (4, 1, DOC_GRP, 1), jnp.float32, 0.0, math.log(10.0)))
    col_scale = jnp.exp(jax.random.uniform(col_key, (1, KSPL, 1, KBLK), jnp.float32, 0.0, math.log(3.0)))
    values = values * row_scale * col_scale * K ** (-0.5)
    return values.reshape(4 * KSPL, DOC_GRP, KBLK).astype(jnp.bfloat16)


def draw_query_grads(key, part):
    key = jax.random.fold_in(key, 23)
    noise_key, row_key = jax.random.split(key, 2)
    values = jax.random.normal(noise_key, (4, KSPL, QRY_GRP, KBLK), jnp.float32)
    growth = 3.0
    values = jnp.clip(values, -6.0, 6.0)
    rows = jnp.arange(4, dtype=jnp.float32)[:, None] * QRY_GRP + jnp.arange(QRY_GRP, dtype=jnp.float32)[None, :]
    position = rows / max(NQ - 1, 1)
    amplitude = jnp.exp(0.5 * math.log(growth) * position).reshape(4, 1, QRY_GRP, 1)
    row_scale = jnp.exp(jax.random.uniform(row_key, (4, 1, QRY_GRP, 1), jnp.float32, 0.0, math.log(10.0))) * amplitude
    values = values * row_scale
    return values.reshape(4 * KSPL, QRY_GRP, KBLK).astype(jnp.bfloat16)


def setup_inputs(seed: int = 0, part: int = 0) -> dict:
    splits = jax.random.split(jax.random.key(seed), 3)
    own_keys = jax.random.split(jax.random.fold_in(splits[2], part), 3)
    return {
        "doc_grads": draw_doc_grads(jax.random.fold_in(jax.random.fold_in(splits[2], part), 71), part),
        "query_grads": draw_query_grads(jax.random.fold_in(jax.random.fold_in(splits[2], part), 71), part),
    }


def reference(doc_grads, query_grads):
    query_tiles = query_grads.reshape(4, KSPL, QRY_GRP, KBLK)
    doc_tiles = doc_grads.reshape(4, KSPL, DOC_GRP, KBLK)

    def add_block(block, total):
        queries = lax.dynamic_index_in_dim(query_tiles, block, 1, keepdims=False).reshape(NQ, KBLK)
        documents = lax.dynamic_index_in_dim(doc_tiles, block, 1, keepdims=False).reshape(NDOC, KBLK)
        return total + jnp.dot(queries, documents.T, preferred_element_type=jnp.float32)
    scores = lax.fori_loop(0, KSPL, add_block, jnp.zeros((NQ, NDOC), jnp.float32))
    spread = lax.optimization_barrier(jnp.mean(scores * scores, axis=0))
    return scores * lax.rsqrt(spread + jnp.float32(1e-06))[None, :]
```

```python
import functools

import jax
import jax.numpy as jnp
from jax import lax
from jax.experimental import pallas as pl
from jax.experimental.pallas import tpu as pltpu
from jax.sharding import PartitionSpec as P

epsilon = 1e-06
groups = 4
chunks = 32
lent = 8
lag = 4
contract = (((1,), (1,)), ((), ()))


def link_phases(parts):
    kept = chunks - lent
    after = lent + parts * lent
    relay = max(after + lag, chunks + lent)
    final = max(relay + lag, 2 * kept)
    table = (
        ((0, lent, False, 0, 0), (lent, parts * lent, True, 0, 0), (after, kept, False, 0, lent)),
        ((0, kept, False, 0, lent), (kept, lent, False, 0, 0), (chunks, lent, False, 1, 0), (relay, kept, False, 1, lent)),
        ((0, kept, False, 0, lent), (kept, kept, False, 1, lent), (final, kept, False, 2, lent)),
    )
    ends = (
        (after + kept - 1,),
        (chunks - 1, relay + kept - 1),
        (kept - 1, 2 * kept - 1, final + kept - 1),
    )
    return table, ends, final + kept, after


def kernel(axis, dims, q_ref, d_ref, out_ref, held, lent_q, qbuf, dbuf, acc, lent_acc, red, lent_red, lent_sum, returned,
           squares, others, load_sem, send_sem, recv_sem, red_send, red_recv, lred_send, lred_recv, ret_send, ret_recv,
           sq_send, sq_recv):
    n, span, rows, docs, cols = dims
    parts = rows // docs
    width = cols // chunks
    share = rows // span
    table, ends, steps, lent_ready = link_phases(parts)
    me = lax.axis_index(axis)
    z = me // span
    b = me - z * span

    def at(index):
        return {axis: index}

    barrier = pltpu.get_barrier_semaphore()

    def greet(o, carry):
        pl.semaphore_signal(barrier, inc=1, device_id=at(lax.rem(me + o, n)), device_id_type=pl.DeviceIdType.MESH)
        return carry

    lax.fori_loop(1, n, greet, 0)
    pl.semaphore_wait(barrier, n - 1)

    def columns(chunk):
        return pl.ds(pl.multiple_of(chunk * width, width), width)

    def item(direction, sender, step):
        place = sender if direction == 0 else groups - 1 - sender
        is_doc = jnp.int32(0)
        is_query = jnp.int32(0)
        back = jnp.int32(0)
        chunk = jnp.int32(0)
        piece = jnp.int32(0)
        last = jnp.int32(0)
        for link, phases in enumerate(table):
            for first, count, query, behind, start in phases:
                hit = ((place == link) & (step >= first) & (step < first + count)).astype(jnp.int32)
                offset = step - first
                if query:
                    is_query = is_query + hit
                    chunk = chunk + hit * (start + offset // parts)
                    piece = piece + hit * (offset % parts)
                else:
                    is_doc = is_doc + hit
                    chunk = chunk + hit * (start + offset)
                    back = back + hit * behind
            for end in ends[link]:
                last = last + ((place == link) & (step == end)).astype(jnp.int32)
        block = sender - back if direction == 0 else sender + back
        return is_doc == 1, is_query == 1, block, chunk, piece, last == 1

    def target(direction):
        return lax.rem(me + (span if direction == 0 else n - span), n)

    def remote(direction, step, source, place):
        return pltpu.make_async_remote_copy(
            src_ref=source,
            dst_ref=place,
            send_sem=send_sem.at[direction, lax.rem(step, lag)],
            recv_sem=recv_sem.at[direction, step],
            device_id=at(target(direction)),
            device_id_type=pl.DeviceIdType.MESH,
        )

    def send(direction, step):
        is_doc, is_query, block, chunk, piece, _ = item(direction, z, step)

        @pl.when(is_doc & (block == z))
        def _():
            remote(direction, step, d_ref.at[:, columns(chunk)], held.at[z, :, columns(chunk)]).start()

        @pl.when(is_doc & (block != z))
        def _():
            remote(direction, step, held.at[block, :, columns(chunk)], held.at[block, :, columns(chunk)]).start()

        @pl.when(is_query)
        def _():
            taken = pl.ds(pl.multiple_of(piece * docs, docs), docs)
            remote(direction, step, q_ref.at[taken, columns(chunk)], lent_q.at[taken, columns(chunk)]).start()

    def wait_sent(direction, step):
        is_doc, is_query, _, _, _, _ = item(direction, z, step)

        @pl.when(is_doc | is_query)
        def _():
            remote(direction, step, d_ref.at[:, columns(0)], held.at[z, :, columns(0)]).wait_send()

    def wait_arrived(direction, step, arriving):
        is_doc, is_query, block, chunk, piece, _ = arriving

        @pl.when(is_doc)
        def _():
            place = held.at[block, :, columns(chunk)]
            remote(direction, step, place, place).wait_recv()

        @pl.when(is_query)
        def _():
            place = lent_q.at[pl.ds(pl.multiple_of(piece * docs, docs), docs), columns(chunk)]
            remote(direction, step, place, place).wait_recv()

    def load_queries(source, chunk, slot):
        return pltpu.make_async_copy(source.at[:, columns(chunk)], qbuf.at[slot], load_sem.at[0, slot])

    def load_documents(block, chunk, slot, start):
        own = pltpu.make_async_copy(d_ref.at[:, columns(chunk)], dbuf.at[slot], load_sem.at[1, slot])
        if not start:
            own.wait()
            return

        @pl.when(block == z)
        def _():
            own.start()

        @pl.when(block != z)
        def _():
            pltpu.make_async_copy(held.at[block, :, columns(chunk)], dbuf.at[slot], load_sem.at[1, slot]).start()

    def reduce_copy(block, o):
        peer = lax.rem(b + o, span)
        return pltpu.make_async_remote_copy(
            src_ref=acc.at[block, pl.ds(pl.multiple_of(peer * share, share), share), :],
            dst_ref=red.at[block, o - 1],
            send_sem=red_send.at[block],
            recv_sem=red_recv.at[block],
            device_id=at(z * span + peer),
            device_id_type=pl.DeviceIdType.MESH,
        )

    def reduce_send(block):
        def one(o, carry):
            reduce_copy(block, o).start()
            return carry

        lax.fori_loop(1, span, one, 0)

    own_rows = pl.ds(pl.multiple_of(b * share, share), share)
    middle = (z == 1) | (z == 2)
    first_lent = jnp.where(z <= 1, 1, 0)
    outward = jnp.where((z == 1) | (z == groups - 1), me - span, me + span)

    def lent_copy(o):
        peer = lax.rem(b + o, span)
        return pltpu.make_async_remote_copy(
            src_ref=lent_acc.at[:, pl.ds(pl.multiple_of(peer * share, share), share), :],
            dst_ref=lent_red.at[o - 1],
            send_sem=lred_send,
            recv_sem=lred_recv,
            device_id=at(z * span + peer),
            device_id_type=pl.DeviceIdType.MESH,
        )

    def return_copy():
        return pltpu.make_async_remote_copy(
            src_ref=lent_sum,
            dst_ref=returned,
            send_sem=ret_send,
            recv_sem=ret_recv,
            device_id=at(outward),
            device_id_type=pl.DeviceIdType.MESH,
        )

    acc[...] = jnp.zeros_like(acc)
    lent_acc[...] = jnp.zeros_like(lent_acc)
    squares[...] = jnp.zeros_like(squares)
    lent_step = lent_ready + lag
    lent_send = lent_step + lent
    lent_back = lent_send + 4

    def step_body(t, carry):
        before = t - lag
        rightward = item(0, z - 1, before)
        leftward = item(1, z + 1, before)
        wait_arrived(0, before, rightward)
        wait_arrived(1, before, leftward)
        for direction in (0, 1):
            wait_sent(direction, before)
            send(direction, t)

        jobs = (
            (rightward[0], rightward[2], rightward[3], rightward[5]),
            (leftward[0], leftward[2], leftward[3], leftward[5]),
            (t < chunks, z, t, t == chunks - 1),
        )
        for slot, (valid, block, chunk, _) in enumerate(jobs):

            @pl.when(valid)
            def _(slot=slot, block=block, chunk=chunk):
                load_queries(q_ref, chunk, slot).start()
                load_documents(block, chunk, slot, True)

        def multiply(slot, carry):
            def pick(which):
                values = [job[which].astype(jnp.int32) for job in jobs]
                return jnp.where(slot == 0, values[0], jnp.where(slot == 1, values[1], values[2]))

            block = pick(1)

            @pl.when(pick(0) == 1)
            def _():
                load_queries(q_ref, 0, slot).wait()
                load_documents(block, 0, slot, False)
                acc[block] += lax.dot_general(qbuf[slot], dbuf[slot], contract, preferred_element_type=jnp.float32)

                @pl.when(pick(3) == 1)
                def _():
                    reduce_send(block)

            return carry

        lax.fori_loop(0, 3, multiply, 0)

        @pl.when(middle & (t >= lent_step) & (t < lent_send))
        def _():
            chunk = t - lent_step
            load_queries(lent_q, chunk, 0).start()
            for j in range(groups - 1):
                load_documents(first_lent + j, chunk, j, True)
            load_queries(lent_q, chunk, 0).wait()

            def one(j, carry):
                load_documents(0, 0, j, False)
                lent_acc[j] += lax.dot_general(qbuf[0], dbuf[j], contract, preferred_element_type=jnp.float32)
                return carry

            lax.fori_loop(0, groups - 1, one, 0)

        @pl.when(middle & (t == lent_send))
        def _():
            def one(o, carry):
                lent_copy(o).start()
                return carry

            lax.fori_loop(1, span, one, 0)

        @pl.when(middle & (t == lent_back))
        def _():
            pltpu.make_async_copy(lent_red, lent_red, lred_recv).wait()
            lent_sum[...] = lent_acc[:, own_rows, :]

            def one(o, carry):
                lent_sum[...] += lent_red[o]
                return carry

            lax.fori_loop(0, span - 1, one, 0)
            return_copy().start()

        return carry

    lax.fori_loop(0, steps + lag, step_body, 0)

    for block in range(groups):
        here = pl.ds(block * docs, docs)
        pltpu.make_async_copy(red.at[block], red.at[block], red_recv.at[block]).wait()
        out_ref[:, here] = acc[block, own_rows, :]

        def one(o, carry):
            out_ref[:, here] += red[block, o]
            return carry

        lax.fori_loop(0, span - 1, one, 0)

    for edge, first in ((0, 1), (groups - 1, 0)):

        @pl.when(z == edge)
        def _(first=first):
            return_copy().wait_recv()
            for j in range(groups - 1):
                out_ref[:, pl.ds((first + j) * docs, docs)] += returned[j]

    for block in range(groups):
        value = out_ref[:, pl.ds(block * docs, docs)]
        squares[pl.ds(block, 1), :] = jnp.sum(value * value, axis=0, keepdims=True)

    def square_copy(o):
        return pltpu.make_async_remote_copy(
            src_ref=squares,
            dst_ref=others.at[o - 1],
            send_sem=sq_send,
            recv_sem=sq_recv,
            device_id=at(lax.rem(me + o, n)),
            device_id_type=pl.DeviceIdType.MESH,
        )

    def tell(o, carry):
        square_copy(o).start()
        return carry

    lax.fori_loop(1, n, tell, 0)
    pltpu.make_async_copy(others, others, sq_recv).wait()
    total = lax.fori_loop(0, n - 1, lambda o, value: value + others[o], squares[...])
    scale = lax.rsqrt(total / (groups * rows) + epsilon)
    for block in range(groups):
        here = pl.ds(block * docs, docs)
        out_ref[:, here] = out_ref[:, here] * scale[block:block + 1, :]

    pltpu.make_async_copy(others, others, sq_send).wait()
    for block in range(groups):
        pltpu.make_async_copy(red.at[block], red.at[block], red_send.at[block]).wait()

    @pl.when(middle)
    def _():
        pltpu.make_async_copy(lent_red, lent_red, lred_send).wait()
        return_copy().wait_send()


def on_device(doc_grads, query_grads):
    doc_tile = doc_grads[0]
    query_tile = query_grads[0]
    n = lax.axis_size("doc")
    span = n // groups
    docs, cols = doc_tile.shape
    rows = query_tile.shape[0]
    width = cols // chunks
    share = rows // span
    any_space = pl.BlockSpec(memory_space=pl.ANY)
    f32, bf16 = jnp.float32, jnp.bfloat16
    dma = pltpu.SemaphoreType.DMA
    steps = link_phases(rows // docs)[2]
    out, _, _ = pl.pallas_call(
        functools.partial(kernel, "doc", (n, span, rows, docs, cols)),
        out_shape=(
            jax.ShapeDtypeStruct((share, groups * docs), f32),
            jax.ShapeDtypeStruct((groups, docs, cols), bf16),
            jax.ShapeDtypeStruct((rows, lent * width), bf16),
        ),
        in_specs=[any_space, any_space],
        out_specs=(pl.BlockSpec(memory_space=pltpu.VMEM), any_space, any_space),
        scratch_shapes=[
            pltpu.VMEM((3, rows, width), bf16),
            pltpu.VMEM((3, docs, width), bf16),
            pltpu.VMEM((groups, rows, docs), f32),
            pltpu.VMEM((groups - 1, rows, docs), f32),
            pltpu.VMEM((groups, span - 1, share, docs), f32),
            pltpu.VMEM((span - 1, groups - 1, share, docs), f32),
            pltpu.VMEM((groups - 1, share, docs), f32),
            pltpu.VMEM((groups - 1, share, docs), f32),
            pltpu.VMEM((8, docs), f32),
            pltpu.VMEM((n - 1, 8, docs), f32),
            dma((2, 3)),
            dma((2, lag)),
            dma((2, steps)),
            dma((groups,)),
            dma((groups,)),
            dma,
            dma,
            dma,
            dma,
            dma,
            dma,
        ],
        compiler_params=pltpu.CompilerParams(
            collective_id=0, has_side_effects=True, vmem_limit_bytes=48 * 1024 * 1024
        ),
    )(query_tile, doc_tile)
    return out


def solution(mesh):
    placed = (P("doc", "grp", None), P("doc", "grp", None))
    return jax.shard_map(
        on_device, mesh=mesh, in_specs=placed, out_specs=P(("grp", "doc"), None), check_vma=False
    )
```

```python
import functools

import jax
import jax.numpy as jnp
from jax import lax
from jax.experimental import pallas as pl
from jax.experimental.pallas import tpu as pltpu
from jax.sharding import PartitionSpec as P

epsilon = 1e-06
groups = 4
most_chunks = 64
lent_share = 9 / 32
lag = 2
contract = (((1,), (1,)), ((), ()))


def cut(cols):
    chunks = min(most_chunks, cols // 128)
    return chunks, int(chunks * lent_share)


def link_phases(parts, chunks, lent):
    kept = chunks - lent
    after = lent + parts * lent
    relay = max(after + lag, chunks + lent)
    final = max(relay + lag, 2 * kept)
    table = (
        ((0, lent, False, 0, 0), (lent, parts * lent, True, 0, 0), (after, kept, False, 0, lent)),
        ((0, kept, False, 0, lent), (kept, lent, False, 0, 0), (chunks, lent, False, 1, 0), (relay, kept, False, 1, lent)),
        ((0, kept, False, 0, lent), (kept, kept, False, 1, lent), (final, kept, False, 2, lent)),
    )
    ends = (
        (after + kept - 1,),
        (chunks - 1, relay + kept - 1),
        (kept - 1, 2 * kept - 1, final + kept - 1),
    )
    return table, ends, final + kept, after


def kernel(axis, dims, q_ref, d_ref, out_ref, held, lent_q, qbuf, dbuf, acc, lent_acc, red, lent_red, lent_sum, returned,
           squares, others, load_sem, send_sem, recv_sem, red_send, red_recv, lred_send, lred_recv, ret_send, ret_recv,
           sq_send, sq_recv):
    n, span, rows, docs, cols = dims
    parts = rows // docs
    chunks, lent = cut(cols)
    width = cols // chunks
    share = rows // span
    table, ends, steps, lent_ready = link_phases(parts, chunks, lent)
    lent_ready = max(lent_ready, chunks + lent)
    me = lax.axis_index(axis)
    z = me // span
    b = me - z * span

    def at(index):
        return {axis: index}

    barrier = pltpu.get_barrier_semaphore()

    def greet(o, carry):
        pl.semaphore_signal(barrier, inc=1, device_id=at(lax.rem(me + o, n)), device_id_type=pl.DeviceIdType.MESH)
        return carry

    lax.fori_loop(1, n, greet, 0)
    pl.semaphore_wait(barrier, n - 1)

    def columns(chunk):
        return pl.ds(pl.multiple_of(chunk * width, width), width)

    def item(direction, sender, step):
        place = sender if direction == 0 else groups - 1 - sender
        is_doc = jnp.int32(0)
        is_query = jnp.int32(0)
        back = jnp.int32(0)
        chunk = jnp.int32(0)
        piece = jnp.int32(0)
        last = jnp.int32(0)
        for link, phases in enumerate(table):
            for first, count, query, behind, start in phases:
                hit = ((place == link) & (step >= first) & (step < first + count)).astype(jnp.int32)
                offset = step - first
                if query:
                    is_query = is_query + hit
                    chunk = chunk + hit * (start + offset // parts)
                    piece = piece + hit * (offset % parts)
                else:
                    is_doc = is_doc + hit
                    chunk = chunk + hit * (start + offset)
                    back = back + hit * behind
            for end in ends[link]:
                last = last + ((place == link) & (step == end)).astype(jnp.int32)
        block = sender - back if direction == 0 else sender + back
        return is_doc == 1, is_query == 1, block, chunk, piece, last == 1

    def target(direction):
        return lax.rem(me + (span if direction == 0 else n - span), n)

    def remote(direction, step, source, place):
        return pltpu.make_async_remote_copy(
            src_ref=source,
            dst_ref=place,
            send_sem=send_sem.at[direction, lax.rem(step, lag)],
            recv_sem=recv_sem.at[direction, step],
            device_id=at(target(direction)),
            device_id_type=pl.DeviceIdType.MESH,
        )

    def send(direction, step):
        is_doc, is_query, block, chunk, piece, _ = item(direction, z, step)

        @pl.when(is_doc & (block == z))
        def _():
            remote(direction, step, d_ref.at[:, columns(chunk)], held.at[z, :, columns(chunk)]).start()

        @pl.when(is_doc & (block != z))
        def _():
            remote(direction, step, held.at[block, :, columns(chunk)], held.at[block, :, columns(chunk)]).start()

        @pl.when(is_query)
        def _():
            taken = pl.ds(pl.multiple_of(piece * docs, docs), docs)
            remote(direction, step, q_ref.at[taken, columns(chunk)], lent_q.at[taken, columns(chunk)]).start()

    def wait_sent(direction, step):
        is_doc, is_query, _, _, _, _ = item(direction, z, step)

        @pl.when(is_doc | is_query)
        def _():
            remote(direction, step, d_ref.at[:, columns(0)], held.at[z, :, columns(0)]).wait_send()

    def wait_arrived(direction, step, arriving):
        is_doc, is_query, block, chunk, piece, _ = arriving

        @pl.when(is_doc)
        def _():
            place = held.at[block, :, columns(chunk)]
            remote(direction, step, place, place).wait_recv()

        @pl.when(is_query)
        def _():
            place = lent_q.at[pl.ds(pl.multiple_of(piece * docs, docs), docs), columns(chunk)]
            remote(direction, step, place, place).wait_recv()

    def load_queries(source, chunk, slot):
        return pltpu.make_async_copy(source.at[:, columns(chunk)], qbuf.at[slot], load_sem.at[0, slot])

    def load_documents(block, chunk, slot, start):
        own = pltpu.make_async_copy(d_ref.at[:, columns(chunk)], dbuf.at[slot], load_sem.at[1, slot])
        if not start:
            own.wait()
            return

        @pl.when(block == z)
        def _():
            own.start()

        @pl.when(block != z)
        def _():
            pltpu.make_async_copy(held.at[block, :, columns(chunk)], dbuf.at[slot], load_sem.at[1, slot]).start()

    def reduce_copy(block, o):
        peer = lax.rem(b + o, span)
        return pltpu.make_async_remote_copy(
            src_ref=acc.at[block, pl.ds(pl.multiple_of(peer * share, share), share), :],
            dst_ref=red.at[block, o - 1],
            send_sem=red_send.at[block],
            recv_sem=red_recv.at[block],
            device_id=at(z * span + peer),
            device_id_type=pl.DeviceIdType.MESH,
        )

    def reduce_send(block):
        def one(o, carry):
            reduce_copy(block, o).start()
            return carry

        lax.fori_loop(1, span, one, 0)

    own_rows = pl.ds(pl.multiple_of(b * share, share), share)
    middle = (z == 1) | (z == 2)
    first_lent = jnp.where(z <= 1, 1, 0)
    outward = jnp.where((z == 1) | (z == groups - 1), me - span, me + span)

    def lent_copy(o):
        peer = lax.rem(b + o, span)
        return pltpu.make_async_remote_copy(
            src_ref=lent_acc.at[:, pl.ds(pl.multiple_of(peer * share, share), share), :],
            dst_ref=lent_red.at[o - 1],
            send_sem=lred_send,
            recv_sem=lred_recv,
            device_id=at(z * span + peer),
            device_id_type=pl.DeviceIdType.MESH,
        )

    def return_copy():
        return pltpu.make_async_remote_copy(
            src_ref=lent_sum,
            dst_ref=returned,
            send_sem=ret_send,
            recv_sem=ret_recv,
            device_id=at(outward),
            device_id_type=pl.DeviceIdType.MESH,
        )

    lent_step = lent_ready + lag
    lent_send = lent_step + lent
    lent_back = lent_send + 4

    def step_body(t, carry):
        before = t - lag
        rightward = item(0, z - 1, before)
        leftward = item(1, z + 1, before)
        wait_arrived(0, before, rightward)
        wait_arrived(1, before, leftward)
        for direction in (0, 1):
            wait_sent(direction, before)
            send(direction, t)

        @pl.when(t == 0)
        def _():
            acc[...] = jnp.zeros_like(acc)
            lent_acc[...] = jnp.zeros_like(lent_acc)
            squares[...] = jnp.zeros_like(squares)

        jobs = (
            (rightward[0], rightward[2], rightward[3], rightward[5]),
            (leftward[0], leftward[2], leftward[3], leftward[5]),
            (t < chunks, z, t, t == chunks - 1),
        )
        for slot, (valid, block, chunk, _) in enumerate(jobs):

            @pl.when(valid)
            def _(slot=slot, block=block, chunk=chunk):
                load_queries(q_ref, chunk, slot).start()
                load_documents(block, chunk, slot, True)

        def multiply(slot, carry):
            def pick(which):
                values = [job[which].astype(jnp.int32) for job in jobs]
                return jnp.where(slot == 0, values[0], jnp.where(slot == 1, values[1], values[2]))

            block = pick(1)

            @pl.when(pick(0) == 1)
            def _():
                load_queries(q_ref, 0, slot).wait()
                load_documents(block, 0, slot, False)
                acc[block] += lax.dot_general(qbuf[slot], dbuf[slot], contract, preferred_element_type=jnp.float32)

                @pl.when(pick(3) == 1)
                def _():
                    reduce_send(block)

            return carry

        lax.fori_loop(0, 3, multiply, 0)

        @pl.when(middle & (t >= lent_step) & (t < lent_send))
        def _():
            chunk = t - lent_step
            load_queries(lent_q, chunk, 0).start()
            for j in range(groups - 1):
                load_documents(first_lent + j, chunk, j, True)
            load_queries(lent_q, chunk, 0).wait()

            def one(j, carry):
                load_documents(0, 0, j, False)
                lent_acc[j] += lax.dot_general(qbuf[0], dbuf[j], contract, preferred_element_type=jnp.float32)
                return carry

            lax.fori_loop(0, groups - 1, one, 0)

        @pl.when(middle & (t == lent_send))
        def _():
            def one(o, carry):
                lent_copy(o).start()
                return carry

            lax.fori_loop(1, span, one, 0)

        @pl.when(middle & (t == lent_back))
        def _():
            pltpu.make_async_copy(lent_red, lent_red, lred_recv).wait()
            lent_sum[...] = lent_acc[:, own_rows, :]

            def one(o, carry):
                lent_sum[...] += lent_red[o]
                return carry

            lax.fori_loop(0, span - 1, one, 0)
            return_copy().start()

        return carry

    lax.fori_loop(0, steps + lag, step_body, 0)

    for block in range(groups):
        here = pl.ds(block * docs, docs)
        pltpu.make_async_copy(red.at[block], red.at[block], red_recv.at[block]).wait()
        out_ref[:, here] = acc[block, own_rows, :]

        def one(o, carry):
            out_ref[:, here] += red[block, o]
            return carry

        lax.fori_loop(0, span - 1, one, 0)

    for edge, first in ((0, 1), (groups - 1, 0)):

        @pl.when(z == edge)
        def _(first=first):
            return_copy().wait_recv()
            for j in range(groups - 1):
                out_ref[:, pl.ds((first + j) * docs, docs)] += returned[j]

    for block in range(groups):
        value = out_ref[:, pl.ds(block * docs, docs)]
        squares[pl.ds(block, 1), :] = jnp.sum(value * value, axis=0, keepdims=True)

    def square_copy(o):
        return pltpu.make_async_remote_copy(
            src_ref=squares,
            dst_ref=others.at[o - 1],
            send_sem=sq_send,
            recv_sem=sq_recv,
            device_id=at(lax.rem(me + o, n)),
            device_id_type=pl.DeviceIdType.MESH,
        )

    def tell(o, carry):
        square_copy(o).start()
        return carry

    lax.fori_loop(1, n, tell, 0)
    pltpu.make_async_copy(others, others, sq_recv).wait()
    total = lax.fori_loop(0, n - 1, lambda o, value: value + others[o], squares[...])
    scale = lax.rsqrt(total / (groups * rows) + epsilon)
    for block in range(groups):
        here = pl.ds(block * docs, docs)
        out_ref[:, here] = out_ref[:, here] * scale[block:block + 1, :]

    pltpu.make_async_copy(others, others, sq_send).wait()
    for block in range(groups):
        pltpu.make_async_copy(red.at[block], red.at[block], red_send.at[block]).wait()

    @pl.when(middle)
    def _():
        pltpu.make_async_copy(lent_red, lent_red, lred_send).wait()
        return_copy().wait_send()


def on_device(doc_grads, query_grads):
    doc_tile = doc_grads[0]
    query_tile = query_grads[0]
    n = lax.axis_size("doc")
    span = n // groups
    docs, cols = doc_tile.shape
    rows = query_tile.shape[0]
    chunks, lent = cut(cols)
    width = cols // chunks
    share = rows // span
    any_space = pl.BlockSpec(memory_space=pl.ANY)
    f32, bf16 = jnp.float32, jnp.bfloat16
    dma = pltpu.SemaphoreType.DMA
    steps = link_phases(rows // docs, chunks, lent)[2]
    out, _, _ = pl.pallas_call(
        functools.partial(kernel, "doc", (n, span, rows, docs, cols)),
        out_shape=(
            jax.ShapeDtypeStruct((share, groups * docs), f32),
            jax.ShapeDtypeStruct((groups, docs, cols), bf16),
            jax.ShapeDtypeStruct((rows, lent * width), bf16),
        ),
        in_specs=[any_space, any_space],
        out_specs=(pl.BlockSpec(memory_space=pltpu.VMEM), any_space, any_space),
        scratch_shapes=[
            pltpu.VMEM((3, rows, width), bf16),
            pltpu.VMEM((3, docs, width), bf16),
            pltpu.VMEM((groups, rows, docs), f32),
            pltpu.VMEM((groups - 1, rows, docs), f32),
            pltpu.VMEM((groups, span - 1, share, docs), f32),
            pltpu.VMEM((span - 1, groups - 1, share, docs), f32),
            pltpu.VMEM((groups - 1, share, docs), f32),
            pltpu.VMEM((groups - 1, share, docs), f32),
            pltpu.VMEM((8, docs), f32),
            pltpu.VMEM((n - 1, 8, docs), f32),
            dma((2, 3)),
            dma((2, lag)),
            dma((2, steps)),
            dma((groups,)),
            dma((groups,)),
            dma,
            dma,
            dma,
            dma,
            dma,
            dma,
        ],
        compiler_params=pltpu.CompilerParams(
            collective_id=0, has_side_effects=True, vmem_limit_bytes=48 * 1024 * 1024
        ),
    )(query_tile, doc_tile)
    return out


def solution(mesh):
    placed = (P("doc", "grp", None), P("doc", "grp", None))
    return jax.shard_map(
        on_device, mesh=mesh, in_specs=placed, out_specs=P(("grp", "doc"), None), check_vma=False
    )
```
